256 devices in a mesh: dp: 256 (over y, z, x, core).
Axes of the slice: x: 4, y: 4, z: 8, core: 2. Of those that a mesh axis runs over, the one named last changes fastest.
Arguments:
- picture_embeddings: bfloat16 [163840, 1152], P('dp')
- caption_embeddings: bfloat16 [163840, 1152], P('dp')
- scale_exponent: float32 [1], replicated, may hold values from 2.3 to 3.4
- additive_offset: float32 [1], replicated, may hold values from -4 to -1
- opponent_round_shifts: int32 [2], replicated, may hold values from 1 to 128, as said below
Outputs:
- grad_images: bfloat16 [163840, 1152], P('dp')
- grad_texts: bfloat16 [163840, 1152], P('dp')
The draws below stay inside these ranges and needn't reach their ends.
Inputs may be any that keep to these rules, and one draw needn't show every extreme that they name: opponent_round_shifts[0] = 128; the entries are distinct powers of two below 256, so every round pairs each block with a different partner.
All inputs are finite; a program needn't handle non-finite values.
Results may differ from the reference program's by a relative error of at most 0.0071.
Values may be sent and summed in bfloat16 or wider, within the bound.
A program may use at most 64 MiB of HBM per device.

```python
import math
import jax
import jax.numpy as jnp
from jax import lax

D = 1152
ROWS_DEV = 640
ROUNDS = 2
TOKENS = 163840
N_DP = 256


def shared_part(key):
    return jax.random.normal(key, (TOKENS, D), jnp.float32)


def embed_draw(key, common):
    noise = jax.random.normal(key, (TOKENS, D), jnp.float32)
    values = 0.45 * common + noise
    return (values / math.sqrt(D)).astype(jnp.bfloat16)


def draw_picture_embeddings(key, part):
    common = shared_part(key)
    key = jax.random.fold_in(key, 1)
    return embed_draw(key, common)


def draw_caption_embeddings(key, part):
    common = shared_part(key)
    key = jax.random.fold_in(key, 2)
    return embed_draw(key, common)


def draw_opponent_round_shifts(key, part):
    key = jax.random.fold_in(key, 3)
    levels = N_DP.bit_length() - 1
    order = jax.random.permutation(key, levels - 1)[:ROUNDS - 1].astype(jnp.int32)
    chosen = jnp.concatenate([jnp.full((1,), levels - 1, jnp.int32), order])
    return jnp.left_shift(jnp.ones((ROUNDS,), jnp.int32), chosen)


def setup_inputs(seed: int = 0) -> dict:
    keys = jax.random.split(jax.random.key(seed), 6)
    return {
        "picture_embeddings": draw_picture_embeddings(jax.random.fold_in(keys[5], 71), 0),
        "caption_embeddings": draw_caption_embeddings(jax.random.fold_in(keys[5], 71), 0),
        "scale_exponent": jnp.clip(jax.random.uniform(keys[2], (1,), jnp.float32, 2.3, 3.4), 2.3, 3.4),
        "additive_offset": jnp.clip(jax.random.uniform(keys[3], (1,), jnp.float32, -4.0, -1.0), -4.0, -1.0),
        "opponent_round_shifts": draw_opponent_round_shifts(jax.random.fold_in(keys[5], 71), 0),
    }


def normalize(values):
    wide = values.astype(jnp.float32)
    norms = jnp.sqrt(lax.optimization_barrier(jnp.sum(wide * wide, axis=-1, keepdims=True)) + 1e-06)
    return ((wide / norms).astype(jnp.bfloat16), norms)

def evaluate_derivatives(picture_embedding_group, caption_embedding_group, score_scale_factor, score_offset_value, matching_pair_indicator):
    similarity_score_table = score_scale_factor * lax.dot_general(picture_embedding_group, caption_embedding_group, (((1,), (1,)), ((), ())), preferred_element_type=jnp.float32) + score_offset_value
    sig = jax.nn.sigmoid(similarity_score_table)
    if matching_pair_indicator:
        sig = sig - jnp.eye(sig.shape[0], dtype=jnp.float32)
    return sig.astype(jnp.bfloat16)

def back_norm(values, norms, grad_unit):
    unit_wide = values.astype(jnp.float32) / norms
    inner = lax.optimization_barrier(jnp.sum(unit_wide * grad_unit, axis=-1, keepdims=True))
    return ((grad_unit - unit_wide * inner) / norms).astype(jnp.bfloat16)

def reference(picture_embeddings, caption_embeddings, scale_exponent, additive_offset, opponent_round_shifts):
    score_scale_factor = jnp.exp(scale_exponent[0])
    score_offset_value = additive_offset[0]
    picture_normed_embeddings, img_norm = normalize(picture_embeddings)
    caption_normed_embeddings, txt_norm = normalize(caption_embeddings)
    blocks = TOKENS // ROWS_DEV
    img_blocks = picture_normed_embeddings.reshape(blocks, ROWS_DEV, D)
    txt_blocks = caption_normed_embeddings.reshape(blocks, ROWS_DEV, D)
    block_ids = jnp.arange(blocks, dtype=jnp.int32)
    partners = [jnp.bitwise_xor(block_ids, opponent_round_shifts[turn].astype(jnp.int32)) for turn in range(ROUNDS)]
    partner_table = jnp.stack(partners, axis=1)

    def per_block(inputs):
        block, partner_row = inputs
        picture_embedding_group = img_blocks[block]
        caption_embedding_group = txt_blocks[block]
        logistic_derivative = evaluate_derivatives(picture_embedding_group, caption_embedding_group, score_scale_factor, score_offset_value, True)
        picture_embedding_derivative = score_scale_factor * jnp.dot(logistic_derivative, caption_embedding_group, preferred_element_type=jnp.float32)
        caption_embedding_derivative = score_scale_factor * lax.dot_general(logistic_derivative, picture_embedding_group, (((0,), (0,)), ((), ())), preferred_element_type=jnp.float32)
        pieces = []
        for turn in range(ROUNDS):
            opponent_caption_group = txt_blocks[partner_row[turn]]
            pairwise_similarity_scores = evaluate_derivatives(picture_embedding_group, opponent_caption_group, score_scale_factor, score_offset_value, False)
            picture_embedding_derivative = picture_embedding_derivative + score_scale_factor * jnp.dot(pairwise_similarity_scores, opponent_caption_group, preferred_element_type=jnp.float32)
            objective_share = score_scale_factor * lax.dot_general(pairwise_similarity_scores, picture_embedding_group, (((0,), (0,)), ((), ())), preferred_element_type=jnp.float32)
            pieces.append(objective_share.astype(jnp.bfloat16))
        return (picture_embedding_derivative, caption_embedding_derivative, jnp.stack(pieces))
    picture_embedding_derivative, caption_embedding_derivative, pieces = lax.map(per_block, (block_ids, partner_table))
    for turn in range(ROUNDS):
        caption_embedding_derivative = caption_embedding_derivative + pieces[partners[turn], turn].astype(jnp.float32)
    grad_images = back_norm(picture_embeddings, img_norm, picture_embedding_derivative.reshape(TOKENS, D))
    grad_texts = back_norm(caption_embeddings, txt_norm, caption_embedding_derivative.reshape(TOKENS, D))
    return (grad_images, grad_texts)
```

```python
import functools

import jax
import jax.numpy as jnp
from jax import lax
from jax.experimental import pallas as pl
from jax.experimental.pallas import tpu as pltpu
from jax.sharding import PartitionSpec as P

MESH = pl.DeviceIdType.MESH
CHUNK = 64
TILE = 128


def rows_at(index, size):
    return pl.ds(pl.multiple_of(index * size, size), size)


def dot_nt(a, b):
    return lax.dot_general(a, b, (((1,), (1,)), ((), ())), preferred_element_type=jnp.float32)


def dot_tn(a, b):
    return lax.dot_general(a, b, (((0,), (0,)), ((), ())), preferred_element_type=jnp.float32)


def dot_nn(a, b):
    return jnp.dot(a, b, preferred_element_type=jnp.float32)


def inverse_norm(wide):
    return 1.0 / jnp.sqrt(jnp.sum(wide * wide, axis=-1, keepdims=True) + 1e-06)


def back_norm(raw, inverse, grad_unit):
    unit = raw.astype(jnp.float32) * inverse
    inner = jnp.sum(unit * grad_unit, axis=-1, keepdims=True)
    return ((grad_unit - unit * inner) * inverse).astype(jnp.bfloat16)


def kernel(
    n,
    shift,
    scale_ref,
    offset_ref,
    img_in,
    txt_in,
    img_out,
    txt_out,
    img_raw,
    txt_raw,
    img_unit,
    txt_unit,
    img_inv,
    txt_inv,
    held,
    slopes,
    txt_grad,
    part,
    returned,
    img_res,
    txt_res,
    img_load,
    txt_load,
    img_store,
    txt_store,
    text_send,
    text_recv,
    part_send,
    part_recv,
):
    rows = img_in.shape[0]
    chunks, tiles = rows // CHUNK, rows // TILE
    me = lax.axis_index("dp")
    across = me ^ (n // 2)
    near = me ^ shift
    far = me ^ (n // 2) ^ shift
    relayed = shift == n // 4
    first, second = (far, near) if relayed else (across, near)

    def load_text(c):
        at = rows_at(c, CHUNK)
        return pltpu.make_async_copy(txt_in.at[at], txt_raw.at[at], txt_load.at[c])

    def load_image(i):
        at = rows_at(i, TILE)
        return pltpu.make_async_copy(img_in.at[at], img_raw.at[at], img_load.at[i])

    def store_text(c):
        at = rows_at(c, CHUNK)
        return pltpu.make_async_copy(txt_res.at[at], txt_out.at[at], txt_store.at[c])

    def store_image(i):
        at = rows_at(i, TILE)
        return pltpu.make_async_copy(img_res.at[at], img_out.at[at], img_store.at[i])

    def send_text(r, c, source, device):
        at = rows_at(c, CHUNK)
        return pltpu.make_async_remote_copy(
            src_ref=source.at[at],
            dst_ref=held.at[r, at],
            send_sem=text_send.at[r, c],
            recv_sem=text_recv.at[r, c],
            device_id=(device,),
            device_id_type=MESH,
        )

    def send_part(r, c, device):
        at = rows_at(c, CHUNK)
        return pltpu.make_async_remote_copy(
            src_ref=part.at[r, at],
            dst_ref=returned.at[r, at],
            send_sem=part_send.at[r, c],
            recv_sem=part_recv.at[r, c],
            device_id=(device,),
            device_id_type=MESH,
        )

    @pl.loop(0, chunks)
    def _(c):
        load_text(c).start()

    @pl.loop(0, tiles)
    def _(i):
        load_image(i).start()

    barrier = pltpu.get_barrier_semaphore()
    for device in (first, second):
        pl.semaphore_signal(barrier, inc=1, device_id=(device,), device_id_type=MESH)
    pl.semaphore_wait(barrier, 2)

    scale = jnp.exp(jnp.full((1, 1), scale_ref[0], jnp.float32))
    offset = offset_ref[0]

    @pl.loop(0, chunks)
    def _(c):
        at = rows_at(c, CHUNK)
        load_text(c).wait()
        wide = txt_raw[at, :].astype(jnp.float32)
        inverse = inverse_norm(wide)
        txt_inv[at, :] = inverse
        txt_unit[at, :] = (wide * inverse).astype(jnp.bfloat16)
        if not relayed:
            send_text(0, c, txt_unit, first).start()
        send_text(1, c, txt_unit, second).start()

    @pl.loop(0, tiles)
    def _(i):
        at = rows_at(i, TILE)
        load_image(i).wait()
        wide = img_raw[at, :].astype(jnp.float32)
        inverse = inverse_norm(wide)
        img_inv[at, :] = inverse
        img_unit[at, :] = (wide * inverse).astype(jnp.bfloat16)

    @pl.loop(0, tiles)
    def _(i):
        at = rows_at(i, TILE)
        logits = dot_nt(txt_unit[at, :], img_unit[...]) * scale + offset
        slope = 1.0 / (1.0 + jnp.exp(-logits))
        row = lax.broadcasted_iota(jnp.int32, slope.shape, 0) + i * TILE
        column = lax.broadcasted_iota(jnp.int32, slope.shape, 1)
        slope = jnp.where(row == column, slope - 1.0, slope).astype(jnp.bfloat16)
        slopes[0, at, :] = slope
        txt_grad[at, :] = scale * dot_nn(slope, img_unit[...])

    def respond(r, c):
        at = rows_at(c, CHUNK)
        logits = dot_nt(held[r, at, :], img_unit[...]) * scale + offset
        slope = (1.0 / (1.0 + jnp.exp(-logits))).astype(jnp.bfloat16)
        slopes[r + 1, at, :] = slope
        part[r, at, :] = (scale * dot_nn(slope, img_unit[...])).astype(jnp.bfloat16)

    if relayed:

        @pl.loop(0, chunks + 2)
        def _(step):
            @pl.when(step < chunks)
            def _():
                send_text(1, step, txt_unit, second).wait_recv()
                send_text(0, step, held.at[1], first).start()
                respond(1, step)

            @pl.when((step >= 1) & (step < chunks + 1))
            def _():
                c = step - 1
                send_text(0, c, held.at[1], first).wait_recv()
                respond(0, c)
                send_part(0, c, first).start()

            @pl.when(step >= 2)
            def _():
                c = step - 2
                at = rows_at(c, CHUNK)
                send_part(0, c, first).wait_recv()
                total = part[1, at, :].astype(jnp.float32) + returned[0, at, :].astype(jnp.float32)
                part[1, at, :] = total.astype(jnp.bfloat16)
                send_part(1, c, second).start()

    else:

        @pl.loop(0, chunks)
        def _(c):
            for r, device in ((1, second), (0, first)):
                send_text(r, c, txt_unit, device).wait_recv()
                respond(r, c)
                send_part(r, c, device).start()

    @pl.loop(0, tiles)
    def _(i):
        at = rows_at(i, TILE)
        grad = dot_tn(slopes[0, :, at], txt_unit[...])
        grad += dot_tn(slopes[1, :, at], held[0])
        grad += dot_tn(slopes[2, :, at], held[1])
        img_res[at, :] = back_norm(img_raw[at, :], img_inv[at, :], scale * grad)
        store_image(i).start()

    @pl.loop(0, chunks)
    def _(c):
        at = rows_at(c, CHUNK)
        grad = txt_grad[at, :]
        send_part(1, c, second).wait_recv()
        grad += returned[1, at, :].astype(jnp.float32)
        if not relayed:
            send_part(0, c, first).wait_recv()
            grad += returned[0, at, :].astype(jnp.float32)
        txt_res[at, :] = back_norm(txt_raw[at, :], txt_inv[at, :], grad)
        store_text(c).start()

    @pl.loop(0, chunks)
    def _(c):
        for r, device in ((0, first), (1, second)):
            send_text(r, c, txt_unit, device).wait_send()
            send_part(r, c, device).wait_send()
        store_text(c).wait()

    @pl.loop(0, tiles)
    def _(i):
        store_image(i).wait()


def exchange(n, level, img, txt, scale_exponent, additive_offset):
    rows, width = img.shape
    chunks, tiles = rows // CHUNK, rows // TILE
    block = functools.partial(pltpu.VMEM, (rows, width))
    pair = functools.partial(pltpu.VMEM, (2, rows, width))
    return pl.pallas_call(
        functools.partial(kernel, n, 1 << level),
        out_shape=(
            jax.ShapeDtypeStruct((rows, width), jnp.bfloat16),
            jax.ShapeDtypeStruct((rows, width), jnp.bfloat16),
        ),
        in_specs=[pl.BlockSpec(memory_space=pltpu.SMEM)] * 2
        + [pl.BlockSpec(memory_space=pl.ANY)] * 2,
        out_specs=[pl.BlockSpec(memory_space=pl.ANY)] * 2,
        scratch_shapes=[
            block(jnp.bfloat16),
            block(jnp.bfloat16),
            block(jnp.bfloat16),
            block(jnp.bfloat16),
            pltpu.VMEM((rows, 1), jnp.float32),
            pltpu.VMEM((rows, 1), jnp.float32),
            pair(jnp.bfloat16),
            pltpu.VMEM((3, rows, rows), jnp.bfloat16),
            block(jnp.float32),
            pair(jnp.bfloat16),
            pair(jnp.bfloat16),
            block(jnp.bfloat16),
            block(jnp.bfloat16),
            pltpu.SemaphoreType.DMA((tiles,)),
            pltpu.SemaphoreType.DMA((chunks,)),
            pltpu.SemaphoreType.DMA((tiles,)),
            pltpu.SemaphoreType.DMA((chunks,)),
            pltpu.SemaphoreType.DMA((2, chunks)),
            pltpu.SemaphoreType.DMA((2, chunks)),
            pltpu.SemaphoreType.DMA((2, chunks)),
            pltpu.SemaphoreType.DMA((2, chunks)),
        ],
        compiler_params=pltpu.CompilerParams(
            collective_id=level, has_side_effects=True, vmem_limit_bytes=40 * 2**20
        ),
        name=f"exchange_{level}",
    )(scale_exponent, additive_offset, img, txt)


def solution(mesh):
    n = mesh.shape["dp"]
    levels = n.bit_length() - 2

    def step(img, txt, scale_exponent, additive_offset, shifts):
        level = 31 - lax.clz(shifts[1])
        branches = [functools.partial(exchange, n, k) for k in range(levels)]
        return lax.switch(level, branches, img, txt, scale_exponent, additive_offset)

    placed = (P("dp", None), P("dp", None), P(), P(), P())
    return jax.shard_map(
        step,
        mesh=mesh,
        in_specs=placed,
        out_specs=(P("dp", None), P("dp", None)),
        check_vma=False,
    )
```

```python
import functools

import jax
import jax.numpy as jnp
from jax import lax
from jax.experimental import pallas as pl
from jax.experimental.pallas import tpu as pltpu
from jax.sharding import PartitionSpec as P

MESH = pl.DeviceIdType.MESH
TILE = 128
AHEAD = 2
LAG = 2


def rows_at(index, size):
    return pl.ds(pl.multiple_of(index * size, size), size)


def dot_nt(a, b):
    return lax.dot_general(a, b, (((1,), (1,)), ((), ())), preferred_element_type=jnp.float32)


def dot_tn(a, b):
    return lax.dot_general(a, b, (((0,), (0,)), ((), ())), preferred_element_type=jnp.float32)


def dot_nn(a, b):
    return jnp.dot(a, b, preferred_element_type=jnp.float32)


def phase(name, count):
    def run(body):
        with jax.named_scope(name):
            pl.loop(0, count)(body)

    return run


def inverse_norm(wide):
    return 1.0 / jnp.sqrt(jnp.sum(wide * wide, axis=-1, keepdims=True) + 1e-06)


def back_norm(raw, inverse, grad_unit):
    unit = raw.astype(jnp.float32) * inverse
    inner = jnp.sum(unit * grad_unit, axis=-1, keepdims=True)
    return ((grad_unit - unit * inner) * inverse).astype(jnp.bfloat16)


def kernel(
    n,
    shift,
    chunk,
    scale_ref,
    offset_ref,
    img_in,
    txt_in,
    img_out,
    txt_out,
    img_raw,
    txt_raw,
    img_unit,
    txt_unit,
    img_inv,
    txt_inv,
    held,
    slopes,
    txt_grad,
    part,
    returned,
    img_load,
    txt_load,
    text_send,
    text_recv,
    part_send,
    part_recv,
):
    rows = img_in.shape[0]
    chunks, tiles = rows // chunk, rows // TILE
    per = chunks // tiles
    me = lax.axis_index("dp")
    across = me ^ (n // 2)
    near = me ^ shift
    far = me ^ (n // 2) ^ shift
    relayed = shift == n // 4
    first, second = (far, near) if relayed else (across, near)

    def load_text(c):
        at = rows_at(c, chunk)
        return pltpu.make_async_copy(txt_in.at[at], txt_raw.at[at], txt_load.at[c])

    def load_image(i):
        at = rows_at(i, TILE)
        return pltpu.make_async_copy(img_in.at[at], img_raw.at[at], img_load.at[i])

    def send_text(r, c, source, device):
        at = rows_at(c, chunk)
        return pltpu.make_async_remote_copy(
            src_ref=source.at[at],
            dst_ref=held.at[r, at],
            send_sem=text_send.at[r, c],
            recv_sem=text_recv.at[r, c],
            device_id=(device,),
            device_id_type=MESH,
        )

    def send_part(r, c, device):
        at = rows_at(c, chunk)
        return pltpu.make_async_remote_copy(
            src_ref=part.at[r, at],
            dst_ref=returned.at[r, at],
            send_sem=part_send.at[r, c],
            recv_sem=part_recv.at[r, c],
            device_id=(device,),
            device_id_type=MESH,
        )

    @phase("load_text", chunks)
    def _(c):
        load_text(c).start()

    @phase("load_image", tiles)
    def _(i):
        load_image(i).start()

    barrier = pltpu.get_barrier_semaphore()
    for device in (first, second):
        pl.semaphore_signal(barrier, inc=1, device_id=(device,), device_id_type=MESH)

    scale = jnp.exp(jnp.full((1, 1), scale_ref[0], jnp.float32))
    offset = offset_ref[0]

    def normalize_text(c):
        at = rows_at(c, chunk)
        load_text(c).wait()
        wide = txt_raw[at, :].astype(jnp.float32)
        inverse = inverse_norm(wide)
        txt_inv[at, :] = inverse
        txt_unit[at, :] = (wide * inverse).astype(jnp.bfloat16)

    normalize_text(0)
    pl.semaphore_wait(barrier, 2)

    @phase("unit_text", chunks)
    def _(c):
        if not relayed:
            send_text(0, c, txt_unit, first).start()
            send_text(1, c, txt_unit, second).start()
        else:

            @pl.when(c < AHEAD)
            def _():
                send_text(1, c, txt_unit, second).start()

        @pl.when(c + 1 < chunks)
        def _():
            normalize_text(c + 1)

    @phase("unit_image", tiles)
    def _(i):
        at = rows_at(i, TILE)
        load_image(i).wait()
        wide = img_raw[at, :].astype(jnp.float32)
        inverse = inverse_norm(wide)
        img_inv[at, :] = inverse
        img_unit[at, :] = (wide * inverse).astype(jnp.bfloat16)

    @phase("own_block", tiles)
    def _(i):
        at = rows_at(i, TILE)
        logits = dot_nt(txt_unit[at, :], img_unit[...]) * scale + offset
        slope = 1.0 / (1.0 + jnp.exp(-logits))
        row = lax.broadcasted_iota(jnp.int32, slope.shape, 0) + i * TILE
        column = lax.broadcasted_iota(jnp.int32, slope.shape, 1)
        slope = jnp.where(row == column, slope - 1.0, slope).astype(jnp.bfloat16)
        slopes[0, at, :] = slope
        txt_grad[at, :] = scale * dot_nn(slope, img_unit[...])

    def respond(r, c):
        at = rows_at(c, chunk)
        logits = dot_nt(held[r, at, :], img_unit[...]) * scale + offset
        slope = (1.0 / (1.0 + jnp.exp(-logits))).astype(jnp.bfloat16)
        slopes[r + 1, at, :] = slope
        part[r, at, :] = (scale * dot_nn(slope, img_unit[...])).astype(jnp.bfloat16)

    def finish_image(i):
        at = rows_at(i, TILE)
        grad = dot_tn(slopes[0, :, at], txt_unit[...])
        grad += dot_tn(slopes[1, :, at], held[0])
        grad += dot_tn(slopes[2, :, at], held[1])
        img_out[at, :] = back_norm(img_raw[at, :], img_inv[at, :], scale * grad)

    def finish_text(c):
        at = rows_at(c, chunk)
        grad = txt_grad[at, :]
        send_part(1, c, second).wait_recv()
        grad += returned[1, at, :].astype(jnp.float32)
        if not relayed:
            send_part(0, c, first).wait_recv()
            grad += returned[0, at, :].astype(jnp.float32)
        txt_out[at, :] = back_norm(txt_raw[at, :], txt_inv[at, :], grad)

    if relayed:

        @phase("pass_and_answer", chunks + 1)
        def _(step):
            @pl.when(step < chunks)
            def _():
                send_text(1, step, txt_unit, second).wait_recv()
                send_text(0, step, held.at[1], first).start()

                @pl.when(step + AHEAD < chunks)
                def _():
                    send_text(1, step + AHEAD, txt_unit, second).start()

                @pl.when(step == chunks - 1)
                def _():
                    @pl.loop(0, chunks - 2)
                    def _(c):
                        send_part(0, c, first).start()

                respond(1, step)

            @pl.when(step >= 1)
            def _():
                c = step - 1
                send_text(0, c, held.at[1], first).wait_recv()
                respond(0, c)

                @pl.when(c >= chunks - 2)
                def _():
                    send_part(0, c, first).start()

        @phase("sum_terms", chunks + LAG)
        def _(step):
            @pl.when(step < chunks)
            def _():
                at = rows_at(step, chunk)
                send_part(0, step, first).wait_recv()
                total = part[1, at, :].astype(jnp.float32) + returned[0, at, :].astype(jnp.float32)
                part[1, at, :] = total.astype(jnp.bfloat16)
                send_part(1, step, second).start()

            @pl.when((step % per == 0) & (step // per < tiles))
            def _():
                finish_image(step // per)

            @pl.when(step >= LAG)
            def _():
                finish_text(step - LAG)

    else:

        @phase("answer", chunks)
        def _(c):
            for r, device in ((1, second), (0, first)):
                send_text(r, c, txt_unit, device).wait_recv()
                respond(r, c)
                send_part(r, c, device).start()

        @phase("image_grad", tiles)
        def _(i):
            finish_image(i)

        @phase("text_grad", chunks)
        def _(c):
            finish_text(c)

    @phase("drain", chunks)
    def _(c):
        for r, device in ((0, first), (1, second)):
            send_text(r, c, txt_unit, device).wait_send()
            send_part(r, c, device).wait_send()


def exchange(n, level, img, txt, scale_exponent, additive_offset):
    rows, width = img.shape
    chunk = 64 if 1 << level == n // 4 else 128
    chunks, tiles = rows // chunk, rows // TILE
    block = functools.partial(pltpu.VMEM, (rows, width))
    pair = functools.partial(pltpu.VMEM, (2, rows, width))
    return pl.pallas_call(
        functools.partial(kernel, n, 1 << level, chunk),
        out_shape=(
            jax.ShapeDtypeStruct((rows, width), jnp.bfloat16),
            jax.ShapeDtypeStruct((rows, width), jnp.bfloat16),
        ),
        in_specs=[pl.BlockSpec(memory_space=pltpu.SMEM)] * 2
        + [pl.BlockSpec(memory_space=pl.ANY)] * 2,
        out_specs=[pl.BlockSpec(memory_space=pltpu.VMEM)] * 2,
        scratch_shapes=[
            block(jnp.bfloat16),
            block(jnp.bfloat16),
            block(jnp.bfloat16),
            block(jnp.bfloat16),
            pltpu.VMEM((rows, 1), jnp.float32),
            pltpu.VMEM((rows, 1), jnp.float32),
            pair(jnp.bfloat16),
            pltpu.VMEM((3, rows, rows), jnp.bfloat16),
            block(jnp.float32),
            pair(jnp.bfloat16),
            pair(jnp.bfloat16),
            pltpu.SemaphoreType.DMA((tiles,)),
            pltpu.SemaphoreType.DMA((chunks,)),
            pltpu.SemaphoreType.DMA((2, chunks)),
            pltpu.SemaphoreType.DMA((2, chunks)),
            pltpu.SemaphoreType.DMA((2, chunks)),
            pltpu.SemaphoreType.DMA((2, chunks)),
        ],
        compiler_params=pltpu.CompilerParams(
            collective_id=level, has_side_effects=True, vmem_limit_bytes=40 * 2**20
        ),
        name=f"exchange_{level}",
    )(scale_exponent, additive_offset, img, txt)


def put_kernel(img, txt, img_out, txt_out, sems):
    parts = sems.shape[1]
    size = img.shape[0] // parts
    copies = []
    for p in range(parts):
        at = pl.ds(p * size, size)
        for k, (source, target) in enumerate(((img, img_out), (txt, txt_out))):
            copy = pltpu.make_async_copy(source.at[at], target.at[at], sems.at[k, p])
            copy.start()
            copies.append(copy)
    for copy in copies:
        copy.wait()


def put(img, txt):
    whole = jax.ShapeDtypeStruct(img.shape, img.dtype)
    return pl.pallas_call(
        put_kernel,
        out_shape=(whole, whole),
        in_specs=[pl.BlockSpec(memory_space=pl.ANY)] * 2,
        out_specs=[pl.BlockSpec(memory_space=pltpu.HBM)] * 2,
        scratch_shapes=[pltpu.SemaphoreType.DMA((2, 4))],
        compiler_params=pltpu.CompilerParams(vmem_limit_bytes=16 * 2**20),
        name="put",
    )(img, txt)


def solution(mesh):
    n = mesh.shape["dp"]
    levels = n.bit_length() - 2

    def step(img, txt, scale_exponent, additive_offset, shifts):
        level = 31 - lax.clz(shifts[1])
        branches = [functools.partial(exchange, n, k) for k in range(levels)]
        return put(*lax.switch(level, branches, img, txt, scale_exponent, additive_offset))

    placed = (P("dp", None), P("dp", None), P(), P(), P())
    return jax.shard_map(
        step,
        mesh=mesh,
        in_specs=placed,
        out_specs=(P("dp", None), P("dp", None)),
        check_vma=False,
    )
```

```python
import functools

import jax
import jax.numpy as jnp
from jax import lax
from jax.experimental import pallas as pl
from jax.experimental.pallas import tpu as pltpu
from jax.sharding import PartitionSpec as P

MESH = pl.DeviceIdType.MESH
TILE = 128
AHEAD = 4
LAG_TEXT = 6
EARLY = 3
LAG = 4


def rows_at(index, size):
    return pl.ds(pl.multiple_of(index * size, size), size)


def dot_nt(a, b):
    return lax.dot_general(a, b, (((1,), (1,)), ((), ())), preferred_element_type=jnp.float32)


def dot_tn(a, b):
    return lax.dot_general(a, b, (((0,), (0,)), ((), ())), preferred_element_type=jnp.float32)


def dot_nn(a, b):
    return jnp.dot(a, b, preferred_element_type=jnp.float32)


def phase(name, count):
    def run(body):
        with jax.named_scope(name):
            pl.loop(0, count)(body)

    return run


def inverse_norm(wide):
    return 1.0 / jnp.sqrt(jnp.sum(wide * wide, axis=-1, keepdims=True) + 1e-06)


def back_norm(raw, inverse, grad_unit):
    unit = raw.astype(jnp.float32) * inverse
    inner = jnp.sum(unit * grad_unit, axis=-1, keepdims=True)
    return ((grad_unit - unit * inner) * inverse).astype(jnp.bfloat16)


def kernel(
    n,
    shift,
    chunk,
    piece,
    scale_ref,
    offset_ref,
    img_in,
    txt_in,
    img_out,
    txt_out,
    img_raw,
    txt_raw,
    img_unit,
    txt_unit,
    img_inv,
    txt_inv,
    held,
    slopes,
    txt_grad,
    part,
    returned,
    img_load,
    txt_load,
    text_send,
    text_recv,
    part_send,
    part_recv,
):
    rows = img_in.shape[0]
    chunks, pieces, tiles = rows // chunk, rows // piece, rows // TILE
    per = chunk // piece
    me = lax.axis_index("dp")
    across = me ^ (n // 2)
    near = me ^ shift
    far = me ^ (n // 2) ^ shift
    relayed = shift == n // 4
    first, second = (far, near) if relayed else (across, near)

    def load_text(c):
        at = rows_at(c, piece)
        return pltpu.make_async_copy(txt_in.at[at], txt_raw.at[at], txt_load.at[c])

    def load_image(i):
        at = rows_at(i, TILE)
        return pltpu.make_async_copy(img_in.at[at], img_raw.at[at], img_load.at[i])

    def send_text(r, c, source, device):
        at = rows_at(c, piece)
        return pltpu.make_async_remote_copy(
            src_ref=source.at[at],
            dst_ref=held.at[r, at],
            send_sem=text_send.at[r, c],
            recv_sem=text_recv.at[r, c],
            device_id=(device,),
            device_id_type=MESH,
        )

    def send_part(r, c, device):
        at = rows_at(c, piece)
        return pltpu.make_async_remote_copy(
            src_ref=part.at[r, at],
            dst_ref=returned.at[r, at],
            send_sem=part_send.at[r, c],
            recv_sem=part_recv.at[r, c],
            device_id=(device,),
            device_id_type=MESH,
        )

    @phase("load_text", pieces)
    def _(c):
        load_text(c).start()

    @phase("load_image", tiles)
    def _(i):
        load_image(i).start()

    barrier = pltpu.get_barrier_semaphore()
    for device in (first, second):
        pl.semaphore_signal(barrier, inc=1, device_id=(device,), device_id_type=MESH)

    scale = jnp.exp(jnp.full((1, 1), scale_ref[0], jnp.float32))
    offset = offset_ref[0]

    def normalize_text(c):
        at = rows_at(c, piece)
        load_text(c).wait()
        wide = txt_raw[at, :].astype(jnp.float32)
        inverse = inverse_norm(wide)
        txt_inv[at, :] = inverse
        txt_unit[at, :] = (wide * inverse).astype(jnp.bfloat16)

    normalize_text(0)
    pl.semaphore_wait(barrier, 2)

    @phase("unit_text", pieces)
    def _(c):
        if not relayed:
            send_text(0, c, txt_unit, first).start()
            send_text(1, c, txt_unit, second).start()
        else:

            @pl.when(c < AHEAD)
            def _():
                send_text(1, c, txt_unit, second).start()

        @pl.when(c + 1 < pieces)
        def _():
            normalize_text(c + 1)

    @phase("unit_image", tiles)
    def _(i):
        at = rows_at(i, TILE)
        load_image(i).wait()
        wide = img_raw[at, :].astype(jnp.float32)
        inverse = inverse_norm(wide)
        img_inv[at, :] = inverse
        img_unit[at, :] = (wide * inverse).astype(jnp.bfloat16)

    def own_tile(i):
        at = rows_at(i, TILE)
        logits = dot_nt(txt_unit[at, :], img_unit[...]) * scale + offset
        slope = 1.0 / (1.0 + jnp.exp(-logits))
        row = lax.broadcasted_iota(jnp.int32, slope.shape, 0) + i * TILE
        column = lax.broadcasted_iota(jnp.int32, slope.shape, 1)
        slope = jnp.where(row == column, slope - 1.0, slope).astype(jnp.bfloat16)
        slopes[0, at, :] = slope
        txt_grad[at, :] = scale * dot_nn(slope, img_unit[...])

    def respond(r, c):
        at = rows_at(c, chunk)
        logits = dot_nt(held[r, at, :], img_unit[...]) * scale + offset
        slope = (1.0 / (1.0 + jnp.exp(-logits))).astype(jnp.bfloat16)
        slopes[r + 1, at, :] = slope
        part[r, at, :] = (scale * dot_nn(slope, img_unit[...])).astype(jnp.bfloat16)

    def finish_image(i):
        at = rows_at(i, TILE)
        grad = dot_tn(slopes[0, :, at], txt_unit[...])
        grad += dot_tn(slopes[1, :, at], held[0])
        grad += dot_tn(slopes[2, :, at], held[1])
        img_out[at, :] = back_norm(img_raw[at, :], img_inv[at, :], scale * grad)

    def finish_text(c):
        at = rows_at(c, piece)
        grad = txt_grad[at, :]
        send_part(1, c, second).wait_recv()
        grad += returned[1, at, :].astype(jnp.float32)
        if not relayed:
            send_part(0, c, first).wait_recv()
            grad += returned[0, at, :].astype(jnp.float32)
        txt_out[at, :] = back_norm(txt_raw[at, :], txt_inv[at, :], grad)

    if relayed:

        @phase("pass_and_answer", pieces + LAG_TEXT)
        def _(step):
            @pl.when(step < pieces)
            def _():
                send_text(1, step, txt_unit, second).wait_recv()
                send_text(0, step, held.at[1], first).start()

                @pl.when(step + AHEAD < pieces)
                def _():
                    send_text(1, step + AHEAD, txt_unit, second).start()

                @pl.when(step % per == per - 2)
                def _():
                    own_tile(step // per)

                @pl.when(step % per == per - 1)
                def _():
                    respond(1, step // per)

            @pl.when(step >= LAG_TEXT)
            def _():
                p = step - LAG_TEXT
                send_text(0, p, held.at[1], first).wait_recv()

                @pl.when(p % per == per - 1)
                def _():
                    respond(0, p // per)

            @pl.when(step == pieces - 1)
            def _():
                @pl.loop(0, EARLY * per)
                def _(p):
                    send_part(0, p, first).start()

            @pl.when((step >= EARLY * per + LAG_TEXT) & ((step - LAG_TEXT) % per == per - 1))
            def _():
                @pl.loop(0, per)
                def _(k):
                    send_part(0, (step - LAG_TEXT) // per * per + k, first).start()

        @phase("sum_terms", pieces + LAG)
        def _(step):
            @pl.when(step < pieces)
            def _():
                at = rows_at(step, piece)
                send_part(0, step, first).wait_recv()
                total = part[1, at, :].astype(jnp.float32) + returned[0, at, :].astype(jnp.float32)
                part[1, at, :] = total.astype(jnp.bfloat16)
                send_part(1, step, second).start()

            @pl.when((step % per == 0) & (step // per < tiles))
            def _():
                finish_image(step // per)

            @pl.when(step >= LAG)
            def _():
                finish_text(step - LAG)

    else:

        @phase("own_block", tiles)
        def _(i):
            own_tile(i)

        @phase("answer", chunks)
        def _(c):
            for r, device in ((1, second), (0, first)):
                for k in range(per):
                    send_text(r, c * per + k, txt_unit, device).wait_recv()
                respond(r, c)
                for k in range(per):
                    send_part(r, c * per + k, device).start()

        @phase("image_grad", tiles)
        def _(i):
            finish_image(i)

        @phase("text_grad", pieces)
        def _(c):
            finish_text(c)

    @phase("drain", pieces)
    def _(c):
        for r, device in ((0, first), (1, second)):
            send_text(r, c, txt_unit, device).wait_send()
            send_part(r, c, device).wait_send()


def exchange(n, level, img, txt, scale_exponent, additive_offset):
    rows, width = img.shape
    chunk = 128
    piece = 32 if 1 << level == n // 4 else chunk
    pieces, tiles = rows // piece, rows // TILE
    block = functools.partial(pltpu.VMEM, (rows, width))
    pair = functools.partial(pltpu.VMEM, (2, rows, width))
    return pl.pallas_call(
        functools.partial(kernel, n, 1 << level, chunk, piece),
        out_shape=(
            jax.ShapeDtypeStruct((rows, width), jnp.bfloat16),
            jax.ShapeDtypeStruct((rows, width), jnp.bfloat16),
        ),
        in_specs=[pl.BlockSpec(memory_space=pltpu.SMEM)] * 2
        + [pl.BlockSpec(memory_space=pl.ANY)] * 2,
        out_specs=[pl.BlockSpec(memory_space=pltpu.VMEM)] * 2,
        scratch_shapes=[
            block(jnp.bfloat16),
            block(jnp.bfloat16),
            block(jnp.bfloat16),
            block(jnp.bfloat16),
            pltpu.VMEM((rows, 1), jnp.float32),
            pltpu.VMEM((rows, 1), jnp.float32),
            pair(jnp.bfloat16),
            pltpu.VMEM((3, rows, rows), jnp.bfloat16),
            block(jnp.float32),
            pair(jnp.bfloat16),
            pair(jnp.bfloat16),
            pltpu.SemaphoreType.DMA((tiles,)),
            pltpu.SemaphoreType.DMA((pieces,)),
            pltpu.SemaphoreType.DMA((2, pieces)),
            pltpu.SemaphoreType.DMA((2, pieces)),
            pltpu.SemaphoreType.DMA((2, pieces)),
            pltpu.SemaphoreType.DMA((2, pieces)),
        ],
        compiler_params=pltpu.CompilerParams(
            collective_id=level, has_side_effects=True, vmem_limit_bytes=40 * 2**20
        ),
        name=f"exchange_{level}",
    )(scale_exponent, additive_offset, img, txt)


def put_kernel(img, txt, img_out, txt_out, sems):
    parts = sems.shape[1]
    size = img.shape[0] // parts
    copies = []
    for p in range(parts):
        at = pl.ds(p * size, size)
        for k, (source, target) in enumerate(((img, img_out), (txt, txt_out))):
            copy = pltpu.make_async_copy(source.at[at], target.at[at], sems.at[k, p])
            copy.start()
            copies.append(copy)
    for copy in copies:
        copy.wait()


def put(img, txt):
    whole = jax.ShapeDtypeStruct(img.shape, img.dtype)
    return pl.pallas_call(
        put_kernel,
        out_shape=(whole, whole),
        in_specs=[pl.BlockSpec(memory_space=pl.ANY)] * 2,
        out_specs=[pl.BlockSpec(memory_space=pltpu.HBM)] * 2,
        scratch_shapes=[pltpu.SemaphoreType.DMA((2, 4))],
        compiler_params=pltpu.CompilerParams(vmem_limit_bytes=16 * 2**20),
        name="put",
    )(img, txt)


def solution(mesh):
    n = mesh.shape["dp"]
    levels = n.bit_length() - 2

    def step(img, txt, scale_exponent, additive_offset, shifts):
        level = 31 - lax.clz(shifts[1])
        branches = [functools.partial(exchange, n, k) for k in range(levels)]
        return put(*lax.switch(level, branches, img, txt, scale_exponent, additive_offset))

    placed = (P("dp", None), P("dp", None), P(), P(), P())
    return jax.shard_map(
        step,
        mesh=mesh,
        in_specs=placed,
        out_specs=(P("dp", None), P("dp", None)),
        check_vma=False,
    )
```

```python
import functools

import jax
import jax.numpy as jnp
from jax import lax
from jax.experimental import pallas as pl
from jax.experimental.pallas import tpu as pltpu
from jax.sharding import PartitionSpec as P

MESH = pl.DeviceIdType.MESH
TILE = 128
AHEAD = 4
LAG_TEXT = 6
EARLY = 3
LAG = 4


def rows_at(index, size):
    return pl.ds(pl.multiple_of(index * size, size), size)


def dot_nt(a, b):
    return lax.dot_general(a, b, (((1,), (1,)), ((), ())), preferred_element_type=jnp.float32)


def dot_tn(a, b):
    return lax.dot_general(a, b, (((0,), (0,)), ((), ())), preferred_element_type=jnp.float32)


def dot_nn(a, b):
    return jnp.dot(a, b, preferred_element_type=jnp.float32)


def phase(name, count):
    def run(body):
        with jax.named_scope(name):
            pl.loop(0, count)(body)

    return run


def inverse_norm(wide):
    return 1.0 / jnp.sqrt(jnp.sum(wide * wide, axis=-1, keepdims=True) + 1e-06)


def back_norm(raw, inverse, grad_unit):
    unit = raw.astype(jnp.float32) * inverse
    inner = jnp.sum(unit * grad_unit, axis=-1, keepdims=True)
    return ((grad_unit - unit * inner) * inverse).astype(jnp.bfloat16)


def kernel(
    n,
    shift,
    chunk,
    piece,
    text_piece,
    scale_ref,
    offset_ref,
    img_in,
    txt_in,
    img_out,
    txt_out,
    img_raw,
    txt_raw,
    img_unit,
    txt_unit,
    img_inv,
    txt_inv,
    held,
    slopes,
    txt_grad,
    part,
    returned,
    img_load,
    txt_load,
    text_send,
    text_recv,
    part_send,
    part_recv,
):
    rows = img_in.shape[0]
    chunks, pieces, tiles = rows // chunk, rows // piece, rows // TILE
    per = chunk // piece
    text_pieces = rows // text_piece
    me = lax.axis_index("dp")
    across = me ^ (n // 2)
    near = me ^ shift
    far = me ^ (n // 2) ^ shift
    relayed = shift == n // 4
    first, second = (far, near) if relayed else (across, near)

    def load_text(c):
        at = rows_at(c, text_piece)
        return pltpu.make_async_copy(txt_in.at[at], txt_raw.at[at], txt_load.at[c])

    def load_image(i):
        at = rows_at(i, TILE)
        return pltpu.make_async_copy(img_in.at[at], img_raw.at[at], img_load.at[i])

    def send_text(r, c, source, device):
        at = rows_at(c, text_piece)
        return pltpu.make_async_remote_copy(
            src_ref=source.at[at],
            dst_ref=held.at[r, at],
            send_sem=text_send.at[r, c],
            recv_sem=text_recv.at[r, c],
            device_id=(device,),
            device_id_type=MESH,
        )

    def send_part(r, c, device):
        at = rows_at(c, piece)
        return pltpu.make_async_remote_copy(
            src_ref=part.at[r, at],
            dst_ref=returned.at[r, at],
            send_sem=part_send.at[r, c],
            recv_sem=part_recv.at[r, c],
            device_id=(device,),
            device_id_type=MESH,
        )

    barrier = pltpu.get_barrier_semaphore()
    for device in (first, second):
        pl.semaphore_signal(barrier, inc=1, device_id=(device,), device_id_type=MESH)

    @phase("load_text", text_pieces)
    def _(c):
        load_text(c).start()

    @phase("load_image", tiles)
    def _(i):
        load_image(i).start()

    scale = jnp.exp(jnp.full((1, 1), scale_ref[0], jnp.float32))
    offset = offset_ref[0]

    def normalize_text(c):
        at = rows_at(c, text_piece)
        load_text(c).wait()
        wide = txt_raw[at, :].astype(jnp.float32)
        inverse = inverse_norm(wide)
        txt_inv[at, :] = inverse
        txt_unit[at, :] = (wide * inverse).astype(jnp.bfloat16)

    normalize_text(0)
    pl.semaphore_wait(barrier, 2)

    @phase("unit_text", text_pieces)
    def _(c):
        if not relayed:
            send_text(0, c, txt_unit, first).start()
            send_text(1, c, txt_unit, second).start()
        else:

            @pl.when(c < AHEAD)
            def _():
                send_text(1, c, txt_unit, second).start()

        @pl.when(c + 1 < text_pieces)
        def _():
            normalize_text(c + 1)

    @phase("unit_image", tiles)
    def _(i):
        at = rows_at(i, TILE)
        load_image(i).wait()
        wide = img_raw[at, :].astype(jnp.float32)
        inverse = inverse_norm(wide)
        img_inv[at, :] = inverse
        img_unit[at, :] = (wide * inverse).astype(jnp.bfloat16)

    def own_tile(i):
        at = rows_at(i, TILE)
        logits = dot_nt(txt_unit[at, :], img_unit[...]) * scale + offset
        slope = 1.0 / (1.0 + jnp.exp(-logits))
        row = lax.broadcasted_iota(jnp.int32, slope.shape, 0) + i * TILE
        column = lax.broadcasted_iota(jnp.int32, slope.shape, 1)
        slope = jnp.where(row == column, slope - 1.0, slope).astype(jnp.bfloat16)
        slopes[0, at, :] = slope
        txt_grad[at, :] = scale * dot_nn(slope, img_unit[...])

    def respond(r, c):
        at = rows_at(c, chunk)
        logits = dot_nt(held[r, at, :], img_unit[...]) * scale + offset
        slope = (1.0 / (1.0 + jnp.exp(-logits))).astype(jnp.bfloat16)
        slopes[r + 1, at, :] = slope
        part[r, at, :] = (scale * dot_nn(slope, img_unit[...])).astype(jnp.bfloat16)

    def finish_image(i):
        at = rows_at(i, TILE)
        grad = dot_tn(slopes[0, :, at], txt_unit[...])
        grad += dot_tn(slopes[1, :, at], held[0])
        grad += dot_tn(slopes[2, :, at], held[1])
        img_out[at, :] = back_norm(img_raw[at, :], img_inv[at, :], scale * grad)

    def finish_text(c):
        at = rows_at(c, piece)
        grad = txt_grad[at, :]
        send_part(1, c, second).wait_recv()
        grad += returned[1, at, :].astype(jnp.float32)
        if not relayed:
            send_part(0, c, first).wait_recv()
            grad += returned[0, at, :].astype(jnp.float32)
        txt_out[at, :] = back_norm(txt_raw[at, :], txt_inv[at, :], grad)

    if relayed:

        @phase("pass_and_answer", pieces + LAG_TEXT)
        def _(step):
            @pl.when(step < pieces)
            def _():
                send_text(1, step, txt_unit, second).wait_recv()
                send_text(0, step, held.at[1], first).start()

                @pl.when(step + AHEAD < pieces)
                def _():
                    send_text(1, step + AHEAD, txt_unit, second).start()

                @pl.when(step % per == per - 2)
                def _():
                    own_tile(step // per)

                @pl.when(step % per == per - 1)
                def _():
                    respond(1, step // per)

            @pl.when(step >= LAG_TEXT)
            def _():
                p = step - LAG_TEXT
                send_text(0, p, held.at[1], first).wait_recv()

                @pl.when(p % per == per - 1)
                def _():
                    respond(0, p // per)

            @pl.when(step == pieces - 1)
            def _():
                @pl.loop(0, EARLY * per)
                def _(p):
                    send_part(0, p, first).start()

            @pl.when((step >= EARLY * per + LAG_TEXT) & ((step - LAG_TEXT) % per == per - 1))
            def _():
                @pl.loop(0, per)
                def _(k):
                    send_part(0, (step - LAG_TEXT) // per * per + k, first).start()

        @phase("sum_terms", pieces + LAG)
        def _(step):
            @pl.when(step < pieces)
            def _():
                at = rows_at(step, piece)
                send_part(0, step, first).wait_recv()
                total = part[1, at, :].astype(jnp.float32) + returned[0, at, :].astype(jnp.float32)
                part[1, at, :] = total.astype(jnp.bfloat16)
                send_part(1, step, second).start()

            @pl.when((step % per == 0) & (step // per < tiles))
            def _():
                finish_image(step // per)

            @pl.when(step >= LAG)
            def _():
                finish_text(step - LAG)

    else:

        @phase("own_block", tiles)
        def _(i):
            own_tile(i)

        @phase("answer", text_pieces)
        def _(t):
            for r, device in ((1, second), (0, first)):
                send_text(r, t, txt_unit, device).wait_recv()

            @pl.loop(0, text_piece // chunk)
            def _(k):
                c = t * (text_piece // chunk) + k
                for r, device in ((1, second), (0, first)):
                    respond(r, c)
                    send_part(r, c, device).start()

        @phase("image_grad", tiles)
        def _(i):
            finish_image(i)

        @phase("text_grad", pieces)
        def _(c):
            finish_text(c)

    @phase("drain", pieces)
    def _(c):
        for r, device in ((0, first), (1, second)):
            send_part(r, c, device).wait_send()

    @phase("drain_text", text_pieces)
    def _(c):
        for r, device in ((0, first), (1, second)):
            send_text(r, c, txt_unit, device).wait_send()


def exchange(n, level, img, txt, scale_exponent, additive_offset):
    rows, width = img.shape
    if 1 << level == n // 4:
        chunk, piece, text_piece = 128, 32, 32
    else:
        chunk, piece, text_piece = 160, 160, 160
    pieces, text_pieces, tiles = rows // piece, rows // text_piece, rows // TILE
    block = functools.partial(pltpu.VMEM, (rows, width))
    pair = functools.partial(pltpu.VMEM, (2, rows, width))
    return pl.pallas_call(
        functools.partial(kernel, n, 1 << level, chunk, piece, text_piece),
        out_shape=(
            jax.ShapeDtypeStruct((rows, width), jnp.bfloat16),
            jax.ShapeDtypeStruct((rows, width), jnp.bfloat16),
        ),
        in_specs=[pl.BlockSpec(memory_space=pltpu.SMEM)] * 2
        + [pl.BlockSpec(memory_space=pl.ANY)] * 2,
        out_specs=[pl.BlockSpec(memory_space=pltpu.VMEM)] * 2,
        scratch_shapes=[
            block(jnp.bfloat16),
            block(jnp.bfloat16),
            block(jnp.bfloat16),
            block(jnp.bfloat16),
            pltpu.VMEM((rows, 1), jnp.float32),
            pltpu.VMEM((rows, 1), jnp.float32),
            pair(jnp.bfloat16),
            pltpu.VMEM((3, rows, rows), jnp.bfloat16),
            block(jnp.float32),
            pair(jnp.bfloat16),
            pair(jnp.bfloat16),
            pltpu.SemaphoreType.DMA((tiles,)),
            pltpu.SemaphoreType.DMA((text_pieces,)),
            pltpu.SemaphoreType.DMA((2, text_pieces)),
            pltpu.SemaphoreType.DMA((2, text_pieces)),
            pltpu.SemaphoreType.DMA((2, pieces)),
            pltpu.SemaphoreType.DMA((2, pieces)),
        ],
        compiler_params=pltpu.CompilerParams(
            collective_id=level, has_side_effects=True, vmem_limit_bytes=40 * 2**20
        ),
        name=f"exchange_{level}",
    )(scale_exponent, additive_offset, img, txt)


def put_kernel(img, txt, img_out, txt_out, sems):
    copies = [
        pltpu.make_async_copy(img, img_out, sems.at[0]),
        pltpu.make_async_copy(txt, txt_out, sems.at[1]),
    ]
    for copy in copies:
        copy.start()
    for copy in copies:
        copy.wait()


def put(img, txt):
    whole = jax.ShapeDtypeStruct(img.shape, img.dtype)
    return pl.pallas_call(
        put_kernel,
        out_shape=(whole, whole),
        in_specs=[pl.BlockSpec(memory_space=pl.ANY)] * 2,
        out_specs=[pl.BlockSpec(memory_space=pltpu.HBM)] * 2,
        scratch_shapes=[pltpu.SemaphoreType.DMA((2,))],
        compiler_params=pltpu.CompilerParams(vmem_limit_bytes=16 * 2**20),
        name="put",
    )(img, txt)


def solution(mesh):
    n = mesh.shape["dp"]
    levels = n.bit_length() - 2

    def step(img, txt, scale_exponent, additive_offset, shifts):
        level = 31 - lax.clz(shifts[1])
        branches = [functools.partial(exchange, n, k) for k in range(levels)]
        return put(*lax.switch(level, branches, img, txt, scale_exponent, additive_offset))

    placed = (P("dp", None), P("dp", None), P(), P(), P())
    return jax.shard_map(
        step,
        mesh=mesh,
        in_specs=placed,
        out_specs=(P("dp", None), P("dp", None)),
        check_vma=False,
    )
```

```python
import functools

import jax
import jax.numpy as jnp
from jax import lax
from jax.experimental import pallas as pl
from jax.experimental.pallas import tpu as pltpu
from jax.sharding import PartitionSpec as P

MESH = pl.DeviceIdType.MESH
TILE = 128
STRIP = 32
AHEAD = 4
LAG_TEXT = 6
EARLY = 3
LAG = 4


def rows_at(index, size):
    return pl.ds(pl.multiple_of(index * size, size), size)


def dot_nt(a, b):
    return lax.dot_general(a, b, (((1,), (1,)), ((), ())), preferred_element_type=jnp.float32)


def dot_tn(a, b):
    return lax.dot_general(a, b, (((0,), (0,)), ((), ())), preferred_element_type=jnp.float32)


def dot_nn(a, b):
    return jnp.dot(a, b, preferred_element_type=jnp.float32)


def phase(name, count):
    def run(body):
        with jax.named_scope(name):
            pl.loop(0, count)(body)

    return run


def inverse_norm(wide):
    return 1.0 / jnp.sqrt(jnp.sum(wide * wide, axis=-1, keepdims=True) + 1e-06)


def back_norm(raw, inverse, grad_unit):
    unit = raw.astype(jnp.float32) * inverse
    inner = jnp.sum(unit * grad_unit, axis=-1, keepdims=True)
    return ((grad_unit - unit * inner) * inverse).astype(jnp.bfloat16)


def kernel(
    n,
    shift,
    chunk,
    piece,
    text_piece,
    scale_ref,
    offset_ref,
    img_in,
    txt_in,
    img_out,
    txt_out,
    img_raw,
    txt_raw,
    img_unit,
    txt_unit,
    img_inv,
    txt_inv,
    held,
    slopes,
    txt_grad,
    part,
    returned,
    img_load,
    txt_load,
    text_send,
    text_recv,
    part_send,
    part_recv,
):
    rows = img_in.shape[0]
    chunks, pieces, tiles = rows // chunk, rows // piece, rows // TILE
    per = chunk // piece
    text_pieces = rows // text_piece
    me = lax.axis_index("dp")
    across = me ^ (n // 2)
    near = me ^ shift
    far = me ^ (n // 2) ^ shift
    relayed = shift == n // 4
    first, second = (far, near) if relayed else (across, near)

    def load_text(c):
        at = rows_at(c, text_piece)
        return pltpu.make_async_copy(txt_in.at[at], txt_raw.at[at], txt_load.at[c])

    def load_image(i):
        at = rows_at(i, TILE)
        return pltpu.make_async_copy(img_in.at[at], img_raw.at[at], img_load.at[i])

    def send_text(r, c, source, device):
        at = rows_at(c, text_piece)
        return pltpu.make_async_remote_copy(
            src_ref=source.at[at],
            dst_ref=held.at[r, at],
            send_sem=text_send.at[r, c],
            recv_sem=text_recv.at[r, c],
            device_id=(device,),
            device_id_type=MESH,
        )

    def send_part(r, c, device):
        at = rows_at(c, piece)
        return pltpu.make_async_remote_copy(
            src_ref=part.at[r, at],
            dst_ref=returned.at[r, at],
            send_sem=part_send.at[r, c],
            recv_sem=part_recv.at[r, c],
            device_id=(device,),
            device_id_type=MESH,
        )

    barrier = pltpu.get_barrier_semaphore()
    for device in (first, second):
        pl.semaphore_signal(barrier, inc=1, device_id=(device,), device_id_type=MESH)

    @phase("load_text", text_pieces)
    def _(c):
        load_text(c).start()

    @phase("load_image", tiles)
    def _(i):
        load_image(i).start()

    scale = jnp.exp(jnp.full((1, 1), scale_ref[0], jnp.float32))
    offset = offset_ref[0]

    def normalize(raw, inverses, units, begin, count):
        @pl.loop(begin, begin + count)
        def _(k):
            at = rows_at(k, STRIP)
            wide = raw[at, :].astype(jnp.float32)
            inverse = inverse_norm(wide)
            inverses[at, :] = inverse
            units[at, :] = (wide * inverse).astype(jnp.bfloat16)

    def normalize_text(c):
        load_text(c).wait()
        normalize(txt_raw, txt_inv, txt_unit, c * (text_piece // STRIP), text_piece // STRIP)

    normalize_text(0)
    pl.semaphore_wait(barrier, 2)

    @phase("unit_text", text_pieces)
    def _(c):
        if not relayed:
            send_text(0, c, txt_unit, first).start()
            send_text(1, c, txt_unit, second).start()
        else:

            @pl.when(c < AHEAD)
            def _():
                send_text(1, c, txt_unit, second).start()

        @pl.when(c + 1 < text_pieces)
        def _():
            normalize_text(c + 1)

    @phase("unit_image", tiles)
    def _(i):
        load_image(i).wait()
        normalize(img_raw, img_inv, img_unit, i * (TILE // STRIP), TILE // STRIP)

    def own_tile(i):
        at = rows_at(i, TILE)
        logits = dot_nt(txt_unit[at, :], img_unit[...]) * scale + offset
        slope = 1.0 / (1.0 + jnp.exp(-logits))
        row = lax.broadcasted_iota(jnp.int32, slope.shape, 0) + i * TILE
        column = lax.broadcasted_iota(jnp.int32, slope.shape, 1)
        slope = jnp.where(row == column, slope - 1.0, slope).astype(jnp.bfloat16)
        slopes[0, at, :] = slope
        txt_grad[at, :] = scale * dot_nn(slope, img_unit[...])

    def respond(r, c):
        at = rows_at(c, chunk)
        logits = dot_nt(held[r, at, :], img_unit[...]) * scale + offset
        slope = (1.0 / (1.0 + jnp.exp(-logits))).astype(jnp.bfloat16)
        slopes[r + 1, at, :] = slope
        part[r, at, :] = (scale * dot_nn(slope, img_unit[...])).astype(jnp.bfloat16)

    def finish_image(i):
        at = rows_at(i, TILE)
        grad = dot_tn(slopes[0, :, at], txt_unit[...])
        grad += dot_tn(slopes[1, :, at], held[0])
        grad += dot_tn(slopes[2, :, at], held[1])
        img_out[at, :] = back_norm(img_raw[at, :], img_inv[at, :], scale * grad)

    def finish_text(c):
        at = rows_at(c, piece)
        grad = txt_grad[at, :]
        send_part(1, c, second).wait_recv()
        grad += returned[1, at, :].astype(jnp.float32)
        if not relayed:
            send_part(0, c, first).wait_recv()
            grad += returned[0, at, :].astype(jnp.float32)
        txt_out[at, :] = back_norm(txt_raw[at, :], txt_inv[at, :], grad)

    if relayed:

        @phase("pass_and_answer", pieces + LAG_TEXT)
        def _(step):
            @pl.when(step < pieces)
            def _():
                send_text(1, step, txt_unit, second).wait_recv()
                send_text(0, step, held.at[1], first).start()

                @pl.when(step + AHEAD < pieces)
                def _():
                    send_text(1, step + AHEAD, txt_unit, second).start()

                @pl.when(step % per == per - 2)
                def _():
                    own_tile(step // per)

                @pl.when(step % per == per - 1)
                def _():
                    respond(1, step // per)

            @pl.when(step >= LAG_TEXT)
            def _():
                p = step - LAG_TEXT
                send_text(0, p, held.at[1], first).wait_recv()

                @pl.when(p % per == per - 1)
                def _():
                    respond(0, p // per)

            @pl.when(step == pieces - 1)
            def _():
                @pl.loop(0, EARLY * per)
                def _(p):
                    send_part(0, p, first).start()

            @pl.when((step >= EARLY * per + LAG_TEXT) & ((step - LAG_TEXT) % per == per - 1))
            def _():
                @pl.loop(0, per)
                def _(k):
                    send_part(0, (step - LAG_TEXT) // per * per + k, first).start()

        @phase("sum_terms", pieces + LAG)
        def _(step):
            @pl.when(step < pieces)
            def _():
                at = rows_at(step, piece)
                send_part(0, step, first).wait_recv()
                total = part[1, at, :].astype(jnp.float32) + returned[0, at, :].astype(jnp.float32)
                part[1, at, :] = total.astype(jnp.bfloat16)
                send_part(1, step, second).start()

            @pl.when((step % per == 0) & (step // per < tiles))
            def _():
                finish_image(step // per)

            @pl.when(step >= LAG)
            def _():
                finish_text(step - LAG)

    else:

        @phase("own_block", tiles)
        def _(i):
            own_tile(i)

        @phase("answer", text_pieces)
        def _(t):
            for r, device in ((1, second), (0, first)):
                send_text(r, t, txt_unit, device).wait_recv()

            @pl.loop(0, text_piece // chunk)
            def _(k):
                c = t * (text_piece // chunk) + k
                @pl.loop(0, 2)
                def _(j):
                    respond(1 - j, c)
                    send_part(1 - j, c, jnp.where(j == 0, second, first)).start()

        @phase("image_grad", tiles)
        def _(i):
            finish_image(i)

        @phase("text_grad", pieces)
        def _(c):
            finish_text(c)

    @phase("drain", pieces)
    def _(c):
        for r, device in ((0, first), (1, second)):
            send_part(r, c, device).wait_send()

    @phase("drain_text", text_pieces)
    def _(c):
        for r, device in ((0, first), (1, second)):
            send_text(r, c, txt_unit, device).wait_send()


def exchange(n, level, img, txt, scale_exponent, additive_offset):
    rows, width = img.shape
    if 1 << level == n // 4:
        chunk, piece, text_piece = 128, 32, 32
    else:
        chunk, piece, text_piece = 160, 160, 160
    pieces, text_pieces, tiles = rows // piece, rows // text_piece, rows // TILE
    block = functools.partial(pltpu.VMEM, (rows, width))
    pair = functools.partial(pltpu.VMEM, (2, rows, width))
    return pl.pallas_call(
        functools.partial(kernel, n, 1 << level, chunk, piece, text_piece),
        out_shape=(
            jax.ShapeDtypeStruct((rows, width), jnp.bfloat16),
            jax.ShapeDtypeStruct((rows, width), jnp.bfloat16),
        ),
        in_specs=[pl.BlockSpec(memory_space=pltpu.SMEM)] * 2
        + [pl.BlockSpec(memory_space=pl.ANY)] * 2,
        out_specs=[pl.BlockSpec(memory_space=pltpu.VMEM)] * 2,
        scratch_shapes=[
            block(jnp.bfloat16),
            block(jnp.bfloat16),
            block(jnp.bfloat16),
            block(jnp.bfloat16),
            pltpu.VMEM((rows, 1), jnp.float32),
            pltpu.VMEM((rows, 1), jnp.float32),
            pair(jnp.bfloat16),
            pltpu.VMEM((3, rows, rows), jnp.bfloat16),
            block(jnp.float32),
            pair(jnp.bfloat16),
            pair(jnp.bfloat16),
            pltpu.SemaphoreType.DMA((tiles,)),
            pltpu.SemaphoreType.DMA((text_pieces,)),
            pltpu.SemaphoreType.DMA((2, text_pieces)),
            pltpu.SemaphoreType.DMA((2, text_pieces)),
            pltpu.SemaphoreType.DMA((2, pieces)),
            pltpu.SemaphoreType.DMA((2, pieces)),
        ],
        compiler_params=pltpu.CompilerParams(
            collective_id=level, has_side_effects=True, vmem_limit_bytes=40 * 2**20
        ),
        name=f"exchange_{level}",
    )(scale_exponent, additive_offset, img, txt)


def put_kernel(img, txt, img_out, txt_out, sems):
    copies = [
        pltpu.make_async_copy(img, img_out, sems.at[0]),
        pltpu.make_async_copy(txt, txt_out, sems.at[1]),
    ]
    for copy in copies:
        copy.start()
    for copy in copies:
        copy.wait()


def put(img, txt):
    whole = jax.ShapeDtypeStruct(img.shape, img.dtype)
    return pl.pallas_call(
        put_kernel,
        out_shape=(whole, whole),
        in_specs=[pl.BlockSpec(memory_space=pl.ANY)] * 2,
        out_specs=[pl.BlockSpec(memory_space=pltpu.HBM)] * 2,
        scratch_shapes=[pltpu.SemaphoreType.DMA((2,))],
        compiler_params=pltpu.CompilerParams(vmem_limit_bytes=16 * 2**20),
        name="put",
    )(img, txt)


def solution(mesh):
    n = mesh.shape["dp"]
    levels = n.bit_length() - 2

    def step(img, txt, scale_exponent, additive_offset, shifts):
        level = 31 - lax.clz(shifts[1])
        branches = [functools.partial(exchange, n, k) for k in range(levels)]
        return put(*lax.switch(level, branches, img, txt, scale_exponent, additive_offset))

    placed = (P("dp", None), P("dp", None), P(), P(), P())
    return jax.shard_map(
        step,
        mesh=mesh,
        in_specs=placed,
        out_specs=(P("dp", None), P("dp", None)),
        check_vma=False,
    )
```

```python
import functools

import jax
import jax.numpy as jnp
from jax import lax
from jax.experimental import pallas as pl
from jax.experimental.pallas import tpu as pltpu
from jax.sharding import PartitionSpec as P

MESH = pl.DeviceIdType.MESH
TILE = 128
STRIP = 32
AHEAD = 4
LAG_TEXT = 6
EARLY = 3
LAG = 4


def rows_at(index, size):
    return pl.ds(pl.multiple_of(index * size, size), size)


def dot_nt(a, b):
    return lax.dot_general(a, b, (((1,), (1,)), ((), ())), preferred_element_type=jnp.float32)


def dot_tn(a, b):
    return lax.dot_general(a, b, (((0,), (0,)), ((), ())), preferred_element_type=jnp.float32)


def dot_nn(a, b):
    return jnp.dot(a, b, preferred_element_type=jnp.float32)


def phase(name, count):
    def run(body):
        with jax.named_scope(name):
            pl.loop(0, count)(body)

    return run


def inverse_norm(wide):
    return 1.0 / jnp.sqrt(jnp.sum(wide * wide, axis=-1, keepdims=True) + 1e-06)


def back_norm(raw, inverse, grad_unit):
    unit = raw.astype(jnp.float32) * inverse
    inner = jnp.sum(unit * grad_unit, axis=-1, keepdims=True)
    return ((grad_unit - unit * inner) * inverse).astype(jnp.bfloat16)


def kernel(
    n,
    shift,
    chunk,
    piece,
    text_piece,
    scale_ref,
    offset_ref,
    img_in,
    txt_in,
    img_out,
    txt_out,
    img_raw,
    txt_raw,
    img_unit,
    txt_unit,
    img_inv,
    txt_inv,
    held,
    slopes,
    txt_grad,
    part,
    returned,
    img_load,
    txt_load,
    text_send,
    text_recv,
    part_send,
    part_recv,
):
    rows = img_in.shape[0]
    chunks, pieces, tiles = rows // chunk, rows // piece, rows // TILE
    per = chunk // piece
    text_pieces = rows // text_piece
    me = lax.axis_index("dp")
    across = me ^ (n // 2)
    near = me ^ shift
    far = me ^ (n // 2) ^ shift
    relayed = shift == n // 4
    first, second = (far, near) if relayed else (across, near)

    def load_text(c):
        at = rows_at(c, text_piece)
        return pltpu.make_async_copy(txt_in.at[at], txt_raw.at[at], txt_load.at[c])

    def load_image(i):
        at = rows_at(i, TILE)
        return pltpu.make_async_copy(img_in.at[at], img_raw.at[at], img_load.at[i])

    def send_text(r, c, source, device):
        at = rows_at(c, text_piece)
        return pltpu.make_async_remote_copy(
            src_ref=source.at[at],
            dst_ref=held.at[r, at],
            send_sem=text_send.at[r, c],
            recv_sem=text_recv.at[r, c],
            device_id=(device,),
            device_id_type=MESH,
        )

    def send_part(r, c, device):
        at = rows_at(c, piece)
        return pltpu.make_async_remote_copy(
            src_ref=part.at[r, at],
            dst_ref=returned.at[r, at],
            send_sem=part_send.at[r, c],
            recv_sem=part_recv.at[r, c],
            device_id=(device,),
            device_id_type=MESH,
        )

    barrier = pltpu.get_barrier_semaphore()
    for device in (first, second):
        pl.semaphore_signal(barrier, inc=1, device_id=(device,), device_id_type=MESH)

    @phase("load_text", text_pieces)
    def _(c):
        load_text(c).start()

    @phase("load_image", tiles)
    def _(i):
        load_image(i).start()

    scale = jnp.exp(jnp.full((1, 1), scale_ref[0], jnp.float32))
    offset = offset_ref[0]

    def normalize(raw, inverses, units, begin, count):
        @pl.loop(begin, begin + count)
        def _(k):
            at = rows_at(k, STRIP)
            wide = raw[at, :].astype(jnp.float32)
            inverse = inverse_norm(wide)
            inverses[at, :] = inverse
            units[at, :] = (wide * inverse).astype(jnp.bfloat16)

    def normalize_text(c):
        load_text(c).wait()
        normalize(txt_raw, txt_inv, txt_unit, c * (text_piece // STRIP), text_piece // STRIP)

    normalize_text(0)
    pl.semaphore_wait(barrier, 2)

    @phase("unit_text", text_pieces)
    def _(c):
        if not relayed:
            send_text(0, c, txt_unit, first).start()
            send_text(1, c, txt_unit, second).start()
        else:

            @pl.when(c < AHEAD)
            def _():
                send_text(1, c, txt_unit, second).start()

        @pl.when(c + 1 < text_pieces)
        def _():
            normalize_text(c + 1)

    @phase("unit_image", tiles)
    def _(i):
        load_image(i).wait()
        normalize(img_raw, img_inv, img_unit, i * (TILE // STRIP), TILE // STRIP)

    def own_tile(i):
        at = rows_at(i, TILE)
        logits = dot_nt(txt_unit[at, :], img_unit[...]) * scale + offset
        slope = 1.0 / (1.0 + jnp.exp(-logits))
        row = lax.broadcasted_iota(jnp.int32, slope.shape, 0) + i * TILE
        column = lax.broadcasted_iota(jnp.int32, slope.shape, 1)
        slope = jnp.where(row == column, slope - 1.0, slope).astype(jnp.bfloat16)
        slopes[0, at, :] = slope
        txt_grad[at, :] = scale * dot_nn(slope, img_unit[...])

    def respond(r, c):
        at = rows_at(c, chunk)
        logits = dot_nt(held[r, at, :], img_unit[...]) * scale + offset
        slope = (1.0 / (1.0 + jnp.exp(-logits))).astype(jnp.bfloat16)
        slopes[r + 1, at, :] = slope
        part[r, at, :] = (scale * dot_nn(slope, img_unit[...])).astype(jnp.bfloat16)

    def finish_image(i):
        at = rows_at(i, TILE)
        grad = dot_tn(slopes[0, :, at], txt_unit[...])
        grad += dot_tn(slopes[1, :, at], held[0])
        grad += dot_tn(slopes[2, :, at], held[1])
        img_out[at, :] = back_norm(img_raw[at, :], img_inv[at, :], scale * grad)

    def finish_text(c):
        at = rows_at(c, piece)
        grad = txt_grad[at, :]
        send_part(1, c, second).wait_recv()
        grad += returned[1, at, :].astype(jnp.float32)
        if not relayed:
            send_part(0, c, first).wait_recv()
            grad += returned[0, at, :].astype(jnp.float32)
        txt_out[at, :] = back_norm(txt_raw[at, :], txt_inv[at, :], grad)

    if relayed:

        @phase("pass_and_answer", pieces + LAG_TEXT)
        def _(step):
            @pl.when(step < pieces)
            def _():
                send_text(1, step, txt_unit, second).wait_recv()
                send_text(0, step, held.at[1], first).start()

                @pl.when(step + AHEAD < pieces)
                def _():
                    send_text(1, step + AHEAD, txt_unit, second).start()

                @pl.when(step % per == per - 2)
                def _():
                    own_tile(step // per)

                @pl.when(step % per == per - 1)
                def _():
                    respond(1, step // per)

            @pl.when(step >= LAG_TEXT)
            def _():
                p = step - LAG_TEXT
                send_text(0, p, held.at[1], first).wait_recv()

                @pl.when(p % per == per - 1)
                def _():
                    respond(0, p // per)

            @pl.when(step == pieces - 1)
            def _():
                @pl.loop(0, EARLY * per)
                def _(p):
                    send_part(0, p, first).start()

            @pl.when((step >= EARLY * per + LAG_TEXT) & ((step - LAG_TEXT) % per == per - 1))
            def _():
                @pl.loop(0, per)
                def _(k):
                    send_part(0, (step - LAG_TEXT) // per * per + k, first).start()

        @phase("sum_terms", pieces + LAG)
        def _(step):
            @pl.when(step < pieces)
            def _():
                at = rows_at(step, piece)
                send_part(0, step, first).wait_recv()
                total = part[1, at, :].astype(jnp.float32) + returned[0, at, :].astype(jnp.float32)
                part[1, at, :] = total.astype(jnp.bfloat16)
                send_part(1, step, second).start()

            @pl.when((step % per == 0) & (step // per < tiles))
            def _():
                finish_image(step // per)

            @pl.when(step >= LAG)
            def _():
                finish_text(step - LAG)

    else:

        @phase("own_block", tiles)
        def _(i):
            own_tile(i)

        @phase("answer", text_pieces)
        def _(t):
            for r, device in ((1, second), (0, first)):
                send_text(r, t, txt_unit, device).wait_recv()

            @pl.loop(0, text_piece // chunk)
            def _(k):
                c = t * (text_piece // chunk) + k
                @pl.loop(0, 2)
                def _(j):
                    respond(1 - j, c)
                    send_part(1 - j, c, jnp.where(j == 0, second, first)).start()

        @phase("image_grad", tiles)
        def _(i):
            finish_image(i)

        @phase("text_grad", pieces)
        def _(c):
            finish_text(c)

    @phase("drain", pieces)
    def _(c):
        for r, device in ((0, first), (1, second)):
            send_part(r, c, device).wait_send()

    @phase("drain_text", text_pieces)
    def _(c):
        for r, device in ((0, first), (1, second)):
            send_text(r, c, txt_unit, device).wait_send()


def exchange(n, level, img, txt, scale_exponent, additive_offset):
    rows, width = img.shape
    if 1 << level == n // 4:
        chunk, piece, text_piece = 128, 32, 32
    else:
        chunk, piece, text_piece = 128, 128, 128
    pieces, text_pieces, tiles = rows // piece, rows // text_piece, rows // TILE
    block = functools.partial(pltpu.VMEM, (rows, width))
    pair = functools.partial(pltpu.VMEM, (2, rows, width))
    return pl.pallas_call(
        functools.partial(kernel, n, 1 << level, chunk, piece, text_piece),
        out_shape=(
            jax.ShapeDtypeStruct((rows, width), jnp.bfloat16),
            jax.ShapeDtypeStruct((rows, width), jnp.bfloat16),
        ),
        in_specs=[pl.BlockSpec(memory_space=pltpu.SMEM)] * 2
        + [pl.BlockSpec(memory_space=pl.ANY)] * 2,
        out_specs=[pl.BlockSpec(memory_space=pltpu.VMEM)] * 2,
        scratch_shapes=[
            block(jnp.bfloat16),
            block(jnp.bfloat16),
            block(jnp.bfloat16),
            block(jnp.bfloat16),
            pltpu.VMEM((rows, 1), jnp.float32),
            pltpu.VMEM((rows, 1), jnp.float32),
            pair(jnp.bfloat16),
            pltpu.VMEM((3, rows, rows), jnp.bfloat16),
            block(jnp.float32),
            pair(jnp.bfloat16),
            pair(jnp.bfloat16),
            pltpu.SemaphoreType.DMA((tiles,)),
            pltpu.SemaphoreType.DMA((text_pieces,)),
            pltpu.SemaphoreType.DMA((2, text_pieces)),
            pltpu.SemaphoreType.DMA((2, text_pieces)),
            pltpu.SemaphoreType.DMA((2, pieces)),
            pltpu.SemaphoreType.DMA((2, pieces)),
        ],
        compiler_params=pltpu.CompilerParams(
            collective_id=level, has_side_effects=True, vmem_limit_bytes=40 * 2**20
        ),
        name=f"exchange_{level}",
    )(scale_exponent, additive_offset, img, txt)


def put_kernel(img, txt, img_out, txt_out, sems):
    copies = [
        pltpu.make_async_copy(img, img_out, sems.at[0]),
        pltpu.make_async_copy(txt, txt_out, sems.at[1]),
    ]
    for copy in copies:
        copy.start()
    for copy in copies:
        copy.wait()


def put(img, txt):
    whole = jax.ShapeDtypeStruct(img.shape, img.dtype)
    return pl.pallas_call(
        put_kernel,
        out_shape=(whole, whole),
        in_specs=[pl.BlockSpec(memory_space=pl.ANY)] * 2,
        out_specs=[pl.BlockSpec(memory_space=pltpu.HBM)] * 2,
        scratch_shapes=[pltpu.SemaphoreType.DMA((2,))],
        compiler_params=pltpu.CompilerParams(vmem_limit_bytes=16 * 2**20),
        name="put",
    )(img, txt)


def solution(mesh):
    n = mesh.shape["dp"]
    levels = n.bit_length() - 2

    def step(img, txt, scale_exponent, additive_offset, shifts):
        level = 31 - lax.clz(shifts[1])
        branches = [functools.partial(exchange, n, k) for k in range(levels)]
        return put(*lax.switch(level, branches, img, txt, scale_exponent, additive_offset))

    placed = (P("dp", None), P("dp", None), P(), P(), P())
    return jax.shard_map(
        step,
        mesh=mesh,
        in_specs=placed,
        out_specs=(P("dp", None), P("dp", None)),
        check_vma=False,
    )
```
